512 devices in a mesh: ctx: 32 (over y_hi, z), tp: 16 (over x, y_lo, core).
Axes of the slice: x: 4, y: 4 (y_hi: 2, y_lo: 2; y = y_hi * 2 + y_lo), z: 16, core: 2. Of those that a mesh axis runs over, the one named last changes fastest.
Arguments:
- query_branch: bfloat16 [8192, 8192], P('ctx', 'tp'), may hold values from -6 to 6
- value_branch: bfloat16 [8192, 8192], P('ctx', 'tp'), may hold values from -6 to 6
- gate_branch: bfloat16 [8192, 8192], P('ctx', 'tp'), may hold values from -6 to 6
- spectrum_real: bfloat16 [64, 256, 8192], P('ctx', None, 'tp'), may hold values from -5 to 5
- spectrum_imag: bfloat16 [64, 256, 8192], P('ctx', None, 'tp'), may hold values from -5 to 5
- projection: bfloat16 [8192, 8192], P('ctx', 'tp'), may hold values from -0.0625 to 0.0625
Outputs:
- mixed: bfloat16 [8192, 8192], P('ctx', 'tp')
The draws below stay inside these ranges and needn't reach their ends.
All inputs are finite; a program needn't handle non-finite values.
Results may differ from the reference program's by a relative error of at most 0.0092.
Values may be sent and summed in bfloat16 or wider, within the bound.
A program may use at most 64 MiB of HBM per device.

```python
import math
import jax
import jax.numpy as jnp
from jax import lax

D = 8192
TOK_DEV = 256
TOKENS = 8192
FREQS = 16384
N_CTX = 32


def steps_of(key, extent, cuts, smallest, high):
    def one(axis_at, blocks):
        draws = jax.random.uniform(jax.random.fold_in(jax.random.fold_in(key, 6), axis_at), (blocks,), jnp.float32, smallest / len(cuts), high / len(cuts))
        return jnp.repeat(jnp.exp(draws), extent[axis_at] // blocks).reshape((-1,) + (1,) * (len(extent) - axis_at - 1))

    loudness = one(*cuts[0])
    for cut in cuts[1:]:
        loudness = loudness * one(*cut)
    return loudness


def normal_values(key, extent, deviation, limit, cuts=(), kind=jnp.bfloat16):
    drawn = jax.random.normal(key, extent, jnp.float32) * deviation
    if len(cuts) > 0:
        drawn = steps_of(key, extent, cuts, -0.22, 0.18) * drawn
    return jnp.clip(drawn, min=-limit, max=limit).astype(kind)


def setup_inputs(seed: int = 0) -> dict:
    keys = jax.random.split(jax.random.key(seed), 7)
    query_branch = normal_values(keys[0], (TOKENS, D), 1.0, 6.0, ((0, 32), (1, 16)))
    value_branch = normal_values(keys[1], (TOKENS, D), 1.0, 6.0, ((0, 32), (1, 16)))
    gate_branch = normal_values(keys[2], (TOKENS, D), 1.0, 6.0, ((0, 32), (1, 16)))
    spectrum_real = normal_values(keys[3], (2 * N_CTX, TOK_DEV, D), 1.0, 5.0, ((0, 32), (2, 16)))
    spectrum_imag = normal_values(keys[4], (2 * N_CTX, TOK_DEV, D), 1.0, 5.0, ((0, 32), (2, 16)))
    projection = normal_values(keys[5], (D, D), D ** -0.5, 0.0625, ((0, 32), (1, 16)))
    return dict(query_branch=query_branch, value_branch=value_branch, gate_branch=gate_branch, spectrum_real=spectrum_real, spectrum_imag=spectrum_imag, projection=projection)


def cos_sin(index_grid, period):
    angles = index_grid.astype(jnp.float32) * (2.0 * math.pi / period)
    return jnp.cos(angles), jnp.sin(angles)


def mult(form, left, right):
    return jnp.einsum(form, left.astype(jnp.float32), right.astype(jnp.float32), precision=lax.Precision.HIGHEST)


def reference(query_branch, value_branch, gate_branch, spectrum_real, spectrum_imag, projection):
    chan_block = math.gcd(D, 512)
    block_count = D // chan_block
    outer_count = 2 * N_CTX
    signal = (query_branch.astype(jnp.float32) * value_branch.astype(jnp.float32)).astype(jnp.bfloat16)
    signal_stack = signal.reshape(TOKENS, block_count, chan_block).transpose(1, 0, 2)
    real_stack = spectrum_real.reshape(outer_count, TOK_DEV, block_count, chan_block).transpose(2, 0, 1, 3)
    imag_stack = spectrum_imag.reshape(outer_count, TOK_DEV, block_count, chan_block).transpose(2, 0, 1, 3)
    outer_index = jnp.arange(outer_count, dtype=jnp.int32)
    block_index = jnp.arange(N_CTX, dtype=jnp.int32)
    inner_index = jnp.arange(TOK_DEV, dtype=jnp.int32)
    cos_outer, sin_outer = cos_sin(outer_index[:, None] * block_index[None, :], outer_count)
    cos_outer = cos_outer.astype(jnp.bfloat16)
    sin_outer = sin_outer.astype(jnp.bfloat16)
    cos_inner, sin_inner = cos_sin((inner_index[:, None] * inner_index[None, :]) % TOK_DEV, TOK_DEV)
    cos_inner = cos_inner.astype(jnp.bfloat16)
    sin_inner = sin_inner.astype(jnp.bfloat16)
    twid_cos, twid_sin = cos_sin(outer_index[:, None] * inner_index[None, :], FREQS)
    twid_cos = twid_cos[:, :, None]
    twid_sin = twid_sin[:, :, None]

    def one_block(packed):
        signal_part, filter_real, filter_imag = packed
        grid = signal_part.reshape(N_CTX, TOK_DEV, chan_block)
        outer_real = mult("kp,pjc->kjc", cos_outer, grid)
        outer_imag = -mult("kp,pjc->kjc", sin_outer, grid)
        first_real = (outer_real * twid_cos + outer_imag * twid_sin).astype(jnp.bfloat16)
        first_imag = (outer_imag * twid_cos - outer_real * twid_sin).astype(jnp.bfloat16)
        spec_real = mult("kjc,jm->kmc", first_real, cos_inner) + mult("kjc,jm->kmc", first_imag, sin_inner)
        spec_imag = mult("kjc,jm->kmc", first_imag, cos_inner) - mult("kjc,jm->kmc", first_real, sin_inner)
        gain_real = filter_real.astype(jnp.float32)
        gain_imag = filter_imag.astype(jnp.float32)
        filt_real = (spec_real * gain_real - spec_imag * gain_imag).astype(jnp.bfloat16)
        filt_imag = (spec_real * gain_imag + spec_imag * gain_real).astype(jnp.bfloat16)
        back_real = mult("kmc,jm->kjc", filt_real, cos_inner) - mult("kmc,jm->kjc", filt_imag, sin_inner)
        back_imag = mult("kmc,jm->kjc", filt_imag, cos_inner) + mult("kmc,jm->kjc", filt_real, sin_inner)
        second_real = (back_real * twid_cos - back_imag * twid_sin).astype(jnp.bfloat16)
        second_imag = (back_imag * twid_cos + back_real * twid_sin).astype(jnp.bfloat16)
        summed = mult("kp,kjc->pjc", cos_outer, second_real) - mult("kp,kjc->pjc", sin_outer, second_imag)
        conv_part = (summed * (1.0 / FREQS)).astype(jnp.bfloat16)
        return conv_part.reshape(TOKENS, chan_block)

    conv_stack = lax.map(one_block, (signal_stack, real_stack, imag_stack))
    conv = conv_stack.transpose(1, 0, 2).reshape(TOKENS, D)
    gated = (conv.astype(jnp.float32) * gate_branch.astype(jnp.float32)).astype(jnp.bfloat16)
    return jnp.dot(gated, projection, preferred_element_type=jnp.float32).astype(jnp.bfloat16)
```

```python
import functools
import math

import jax
import jax.numpy as jnp
import ml_dtypes
import numpy as np
from jax import lax
from jax.experimental import pallas as pl
from jax.experimental.pallas import tpu as pltpu
from jax.sharding import PartitionSpec as P

MESH = pl.DeviceIdType.MESH
BF = jnp.bfloat16
F32 = jnp.float32


def cos_sin(grid, period):
    angles = grid.astype(np.float32) * np.float32(2.0 * math.pi / period)
    return np.cos(angles), np.sin(angles)


def tables(n, tok, cb):
    outer = 2 * n
    k, p, j = np.arange(outer), np.arange(n), np.arange(tok)
    bf = ml_dtypes.bfloat16
    co, so = (t.astype(bf).astype(np.float32) for t in cos_sin(k[:, None] * p[None, :], outer))
    ci, si = (t.astype(bf).astype(np.float32) for t in cos_sin(j[:, None] * j[None, :] % tok, tok))
    eye = np.eye(cb, dtype=np.float32)
    outer_fwd = np.concatenate([np.kron(co, eye), -np.kron(so, eye)], 0).astype(bf)
    outer_inv = np.ascontiguousarray(outer_fwd.T)
    inner_fwd = np.block([[ci, -si], [si, ci]]).astype(bf)
    inner_inv = np.block([[ci, si], [-si, ci]]).astype(bf)
    twid = np.stack([np.repeat(t, cb, 0) for t in cos_sin(k[:, None] * j[None, :], outer * tok)])
    return outer_fwd, outer_inv, inner_fwd, inner_inv, twid.astype(np.float32)


def peer(step, me, n):
    z_count = n // 2
    half, z = me // z_count, lax.rem(me, z_count)
    flip, u = lax.rem(step, 2), step // 2
    shift = jnp.where(lax.rem(u, 2) == 1, (u + 1) // 2, z_count - u // 2)
    return lax.rem(half + flip, 2) * z_count + lax.rem(z + shift, z_count)


def conv_kernel(
    n,
    q_ref,
    v_ref,
    gate_ref,
    sr_ref,
    si_ref,
    wf_hbm,
    wi_hbm,
    mf_hbm,
    mi_hbm,
    tw_hbm,
    out_ref,
    wf,
    wi,
    mf,
    mi,
    tw,
    sig_tx,
    sig_rx,
    spec_tx,
    spec_rx,
    freq,
    second,
    conv_tx,
    conv_rx,
    gate_t,
    tab_sem,
    send_sem,
    recv_sem,
):
    me = lax.axis_index("ctx")
    tok, chan = q_ref.shape
    cb = chan // n
    rows = 2 * n * cb

    loads = [
        pltpu.make_async_copy(src, dst, tab_sem.at[i])
        for i, (src, dst) in enumerate(
            ((wf_hbm, wf), (wi_hbm, wi), (mf_hbm, mf), (mi_hbm, mi), (tw_hbm, tw))
        )
    ]
    for load in loads:
        load.start()

    barrier = pltpu.get_barrier_semaphore()

    @pl.loop(1, n)
    def _(s):
        pl.semaphore_signal(barrier, inc=1, device_id={"ctx": peer(s, me, n)}, device_id_type=MESH)

    def exchange(kind, tx, rx, dest):
        return pltpu.make_async_remote_copy(
            src_ref=tx.at[dest],
            dst_ref=rx.at[me],
            send_sem=send_sem.at[kind, dest],
            recv_sem=recv_sem.at[kind, me],
            device_id={"ctx": dest},
            device_id_type=MESH,
        )

    def arrival(kind, tx, rx, src):
        return pltpu.make_async_remote_copy(
            src_ref=tx.at[src],
            dst_ref=rx.at[src],
            send_sem=send_sem.at[kind, src],
            recv_sem=recv_sem.at[kind, src],
            device_id={"ctx": src},
            device_id_type=MESH,
        )

    def send_all(kind, tx, rx):
        @pl.loop(1, n)
        def _(s):
            exchange(kind, tx, rx, peer(s, me, n)).start()

    def recv_all(kind, tx, rx):
        @pl.loop(1, n)
        def _(s):
            arrival(kind, tx, rx, peer(s, me, n)).wait_recv()

    def drain(kind, tx, rx):
        @pl.loop(1, n)
        def _(s):
            exchange(kind, tx, rx, peer(s, me, n)).wait_send()

    signal = (q_ref[...].astype(F32) * v_ref[...].astype(F32)).astype(BF)
    sig_tx[...] = signal.T.reshape(n, cb, tok)
    pl.semaphore_wait(barrier, n - 1)
    send_all(0, sig_tx, sig_rx)
    for part, ref in enumerate((sr_ref, si_ref)):
        for k in range(2):
            at = (2 * part + k) * cb
            spec_tx[:, at : at + cb, :] = ref[k].T.reshape(n, cb, tok)
    send_all(1, spec_tx, spec_rx)
    sig_rx[pl.ds(me, 1)] = sig_tx[pl.ds(me, 1)]
    spec_rx[pl.ds(me, 1)] = spec_tx[pl.ds(me, 1)]
    gate_t[...] = gate_ref[...].T
    for load in loads:
        load.wait()

    recv_all(0, sig_tx, sig_rx)
    step = 8 * cb
    chunks = rows // step

    @pl.loop(0, chunks)
    def _(i):
        at = pl.ds(pl.multiple_of(i * step, step), step)
        lower = pl.ds(pl.multiple_of(rows + i * step, step), step)
        grid = sig_rx[...].reshape(n * cb, tok)
        real = jnp.dot(wf[at, :], grid, preferred_element_type=F32)
        imag = jnp.dot(wf[lower, :], grid, preferred_element_type=F32)
        u, w = tw[0, at, :], tw[1, at, :]
        first = jnp.concatenate(
            [(real * u + imag * w).astype(BF), (imag * u - real * w).astype(BF)], axis=1
        )
        freq[at, :] = jnp.dot(first, mf[...], preferred_element_type=F32)

    recv_all(1, spec_tx, spec_rx)

    @pl.loop(0, chunks)
    def _(i):
        at = pl.ds(pl.multiple_of(i * step, step), step)
        lower = pl.ds(pl.multiple_of(rows + i * step, step), step)
        gain = spec_rx[pl.ds(i * 4, 4)].astype(F32)
        gain_r = gain[:, : 2 * cb].reshape(step, tok)
        gain_i = gain[:, 2 * cb :].reshape(step, tok)
        real, imag = freq[at, :tok], freq[at, tok:]
        filt = jnp.concatenate(
            [
                (real * gain_r - imag * gain_i).astype(BF),
                (real * gain_i + imag * gain_r).astype(BF),
            ],
            axis=1,
        )
        back = jnp.dot(filt, mi[...], preferred_element_type=F32)
        real, imag = back[:, :tok], back[:, tok:]
        u, w = tw[0, at, :], tw[1, at, :]
        second[at, :] = (real * u - imag * w).astype(BF)
        second[lower, :] = (imag * u + real * w).astype(BF)

    scale = 1.0 / (2 * n * tok)
    out_step = 4 * cb

    @pl.loop(0, n // 4)
    def _(i):
        at = pl.ds(pl.multiple_of(i * out_step, out_step), out_step)
        conv = jnp.dot(wi[at, :], second[...], preferred_element_type=F32) * scale
        conv_tx[pl.ds(i * 4, 4)] = conv.astype(BF).reshape(4, cb, tok)

    send_all(2, conv_tx, conv_rx)
    conv_rx[pl.ds(me, 1)] = conv_tx[pl.ds(me, 1)]
    recv_all(2, conv_tx, conv_rx)
    gated = conv_rx[...].reshape(chan, tok).astype(F32) * gate_t[...].astype(F32)
    out_ref[...] = gated.astype(BF).T
    drain(0, sig_tx, sig_rx)
    drain(1, spec_tx, spec_rx)
    drain(2, conv_tx, conv_rx)


def gated_conv(n, q, v, gate, sr, si):
    tok, chan = q.shape
    cb = chan // n
    rows = 2 * n * cb
    consts = [jnp.asarray(t) for t in tables(n, tok, cb)]
    vmem = pl.BlockSpec(memory_space=pltpu.VMEM)
    anyspace = pl.BlockSpec(memory_space=pl.ANY)
    return pl.pallas_call(
        functools.partial(conv_kernel, n),
        out_shape=jax.ShapeDtypeStruct((tok, chan), BF),
        in_specs=[vmem] * 5 + [anyspace] * 5,
        out_specs=vmem,
        scratch_shapes=[pltpu.VMEM(t.shape, t.dtype) for t in consts]
        + [
            pltpu.VMEM((n, cb, tok), BF),
            pltpu.VMEM((n, cb, tok), BF),
            pltpu.VMEM((n, 4 * cb, tok), BF),
            pltpu.VMEM((n, 4 * cb, tok), BF),
            pltpu.VMEM((rows, 2 * tok), F32),
            pltpu.VMEM((2 * rows, tok), BF),
            pltpu.VMEM((n, cb, tok), BF),
            pltpu.VMEM((n, cb, tok), BF),
            pltpu.VMEM((chan, tok), BF),
            pltpu.SemaphoreType.DMA((5,)),
            pltpu.SemaphoreType.DMA((3, n)),
            pltpu.SemaphoreType.DMA((3, n)),
        ],
        compiler_params=pltpu.CompilerParams(
            collective_id=0, has_side_effects=True, vmem_limit_bytes=48 << 20
        ),
        cost_estimate=pl.CostEstimate(
            flops=2 * 10**9, bytes_accessed=10 << 20, transcendentals=0
        ),
    )(q, v, gate, sr, si, *consts)


def local(query_branch, value_branch, gate_branch, spectrum_real, spectrum_imag, projection):
    n = lax.axis_size("ctx")
    gated = gated_conv(n, query_branch, value_branch, gate_branch, spectrum_real, spectrum_imag)
    weights = lax.all_gather(projection, "ctx", axis=0, tiled=True)
    features = lax.all_gather(gated, "tp", axis=1, tiled=True)
    return jnp.dot(features, weights, preferred_element_type=F32).astype(BF)


def solution(mesh):
    return jax.shard_map(
        local,
        mesh=mesh,
        in_specs=(
            P("ctx", "tp"),
            P("ctx", "tp"),
            P("ctx", "tp"),
            P("ctx", None, "tp"),
            P("ctx", None, "tp"),
            P("ctx", "tp"),
        ),
        out_specs=P("ctx", "tp"),
        check_vma=False,
    )
```

```python
import functools
import math

import jax
import jax.numpy as jnp
import ml_dtypes
import numpy as np
from jax import lax
from jax.experimental import pallas as pl
from jax.experimental.pallas import tpu as pltpu
from jax.sharding import PartitionSpec as P

MESH = pl.DeviceIdType.MESH
BF = jnp.bfloat16
F32 = jnp.float32
Y_LOW = 2
CORES = 2
EARLY = 3
MIDDLE = 1


def cos_sin(grid, period):
    angles = grid.astype(np.float32) * np.float32(2.0 * math.pi / period)
    return np.cos(angles), np.sin(angles)


def tables(n, tok, cb):
    outer = 2 * n
    k, p, j = np.arange(outer), np.arange(n), np.arange(tok)
    bf = ml_dtypes.bfloat16
    co, so = (t.astype(bf).astype(np.float32) for t in cos_sin(k[:, None] * p[None, :], outer))
    ci, si = (t.astype(bf).astype(np.float32) for t in cos_sin(j[:, None] * j[None, :] % tok, tok))
    eye = np.eye(cb, dtype=np.float32)
    outer_fwd = np.concatenate([np.kron(co, eye), -np.kron(so, eye)], 0).astype(bf)
    outer_inv = np.ascontiguousarray(outer_fwd.T)
    inner_fwd = np.block([[ci, -si], [si, ci]]).astype(bf)
    inner_inv = np.block([[ci, si], [-si, ci]]).astype(bf)
    twid = np.stack([np.repeat(t, cb, 0) for t in cos_sin(k[:, None] * j[None, :], outer * tok)])
    return outer_fwd, outer_inv, inner_fwd, inner_inv, twid.astype(np.float32)


def peer(step, me, n):
    z_count = n // 2
    half, z = me // z_count, lax.rem(me, z_count)
    flip, u = lax.rem(step, 2), step // 2
    shift = jnp.where(lax.rem(u, 2) == 1, (u + 1) // 2, z_count - u // 2)
    return lax.rem(half + flip, 2) * z_count + lax.rem(z + shift, z_count)


def layer_kernel(
    n,
    groups,
    q_hbm,
    v_hbm,
    gate_hbm,
    sr_hbm,
    si_hbm,
    proj_hbm,
    wf_hbm,
    wi_hbm,
    mf_hbm,
    mi_hbm,
    tw_hbm,
    out_ref,
    q_ref,
    v_ref,
    gate_ref,
    sr_ref,
    si_ref,
    wf,
    wi,
    mf,
    mi,
    tw,
    sig_tx,
    sig_rx,
    spec_tx,
    spec_rx,
    freq,
    second,
    conv_tx,
    conv_rx,
    gate_t,
    weights,
    feat_tx,
    feats,
    part_tx,
    part_rx,
    load_sem,
    send_sem,
    recv_sem,
    w_send,
    w_recv,
    f_send,
    f_recv,
    pair_sem,
):
    me = lax.axis_index("ctx")
    mine = lax.axis_index("tp")
    tok, chan = q_ref.shape
    cb = chan // n
    rows = 2 * n * cb
    z_count = n // 2
    half, z = me // z_count, lax.rem(me, z_count)
    partner = (1 - half) * z_count + z
    x_count = groups // (Y_LOW * CORES)
    core = lax.rem(mine, CORES)
    y_low = lax.rem(mine // CORES, Y_LOW)
    x = mine // (CORES * Y_LOW)
    half_rows = proj_hbm.shape[0] // 2

    def group_at(dx, dy, dc):
        return (
            lax.rem(x + dx + x_count, x_count) * Y_LOW + lax.rem(y_low + dy, Y_LOW)
        ) * CORES + lax.rem(core + dc, CORES)

    near = []
    if x_count > 1:
        near += [group_at(1, 0, 0), group_at(-1, 0, 0)]
    if Y_LOW > 1:
        near.append(group_at(0, 1, 0))
    if CORES > 1:
        near.append(group_at(0, 0, 1))

    pairs = (
        (q_hbm, q_ref),
        (v_hbm, v_ref),
        (proj_hbm.at[pl.ds(pl.multiple_of(half * half_rows, half_rows), half_rows)], weights.at[me]),
        (sr_hbm, sr_ref),
        (si_hbm, si_ref),
        (gate_hbm, gate_ref),
        (wf_hbm, wf),
        (tw_hbm, tw),
        (mf_hbm, mf),
        (mi_hbm, mi),
        (wi_hbm, wi),
    )
    loads = [pltpu.make_async_copy(a, b, load_sem.at[i]) for i, (a, b) in enumerate(pairs)]
    for load in loads:
        load.start()

    barrier = pltpu.get_barrier_semaphore()

    @pl.loop(1, n)
    def _(s):
        pl.semaphore_signal(barrier, inc=1, device_id={"ctx": peer(s, me, n)}, device_id_type=MESH)

    for other in near:
        pl.semaphore_signal(barrier, inc=1, device_id={"tp": other}, device_id_type=MESH)

    def exchange(kind, tx, rx, dest):
        return pltpu.make_async_remote_copy(
            src_ref=tx.at[dest],
            dst_ref=rx.at[me],
            send_sem=send_sem.at[kind, dest],
            recv_sem=recv_sem.at[kind, me],
            device_id={"ctx": dest},
            device_id_type=MESH,
        )

    def arrival(kind, tx, rx, src):
        return pltpu.make_async_remote_copy(
            src_ref=tx.at[src],
            dst_ref=rx.at[src],
            send_sem=send_sem.at[kind, src],
            recv_sem=recv_sem.at[kind, src],
            device_id={"ctx": src},
            device_id_type=MESH,
        )

    def send_all(kind, tx, rx):
        @pl.loop(1, n)
        def _(s):
            exchange(kind, tx, rx, peer(s, me, n)).start()

    def recv_all(kind, tx, rx):
        @pl.loop(1, n)
        def _(s):
            arrival(kind, tx, rx, peer(s, me, n)).wait_recv()

    def drain(kind, tx, rx):
        @pl.loop(1, n)
        def _(s):
            exchange(kind, tx, rx, peer(s, me, n)).wait_send()

    def reach(kind, way):
        return z_count // 2 - (kind + way) % 2

    def ring_copy(kind, way, d):
        sign = 1 - 2 * way
        owner = (half if kind == 0 else 1 - half) * z_count + lax.rem(
            z - sign * d + z_count, z_count
        )
        dest = half * z_count + lax.rem(z + sign + z_count, z_count)
        return pltpu.make_async_remote_copy(
            src_ref=weights.at[owner],
            dst_ref=weights.at[owner],
            send_sem=w_send.at[way, owner],
            recv_sem=w_recv.at[owner],
            device_id={"ctx": dest},
            device_id_type=MESH,
        )

    def ring_step(d):
        for way in range(2):
            for kind in range(2):
                if 1 <= d <= reach(kind, way):
                    ring_copy(kind, way, d).wait_recv()
                if d < reach(kind, way):
                    ring_copy(kind, way, d).start()

    last_step = z_count // 2
    lend = pltpu.make_async_remote_copy(
        src_ref=proj_hbm.at[pl.ds(pl.multiple_of((1 - half) * half_rows, half_rows), half_rows)],
        dst_ref=weights.at[me],
        send_sem=pair_sem.at[0],
        recv_sem=w_recv.at[me],
        device_id={"ctx": partner},
        device_id_type=MESH,
    )

    loads[0].wait()
    loads[1].wait()
    signal = (q_ref[...].astype(F32) * v_ref[...].astype(F32)).astype(BF)
    sig_tx[...] = signal.T.reshape(n, cb, tok)
    pl.semaphore_wait(barrier, n - 1 + len(near))
    send_all(0, sig_tx, sig_rx)
    lend.start()
    loads[3].wait()
    loads[4].wait()
    for part, ref in enumerate((sr_ref, si_ref)):
        for k in range(2):
            at = (2 * part + k) * cb
            spec_tx[:, at : at + cb, :] = ref[k].T.reshape(n, cb, tok)
    send_all(1, spec_tx, spec_rx)
    loads[2].wait()
    ring_copy(1, 0, 0).wait_recv()
    ring_step(0)
    sig_rx[pl.ds(me, 1)] = sig_tx[pl.ds(me, 1)]
    spec_rx[pl.ds(me, 1)] = spec_tx[pl.ds(me, 1)]
    loads[5].wait()
    gate_t[...] = gate_ref[...].T.reshape(n, cb, tok)
    for load in loads[6:]:
        load.wait()

    recv_all(0, sig_tx, sig_rx)
    step = 8 * cb
    chunks = rows // step

    @pl.loop(0, chunks)
    def _(i):
        at = pl.ds(pl.multiple_of(i * step, step), step)
        lower = pl.ds(pl.multiple_of(rows + i * step, step), step)
        grid = sig_rx[...].reshape(n * cb, tok)
        real = jnp.dot(wf[at, :], grid, preferred_element_type=F32)
        imag = jnp.dot(wf[lower, :], grid, preferred_element_type=F32)
        u, w = tw[0, at, :], tw[1, at, :]
        first = jnp.concatenate(
            [(real * u + imag * w).astype(BF), (imag * u - real * w).astype(BF)], axis=1
        )
        freq[at, :] = jnp.dot(first, mf[...], preferred_element_type=F32)

    early = min(EARLY, last_step)
    for d in range(1, early + 1):
        ring_step(d)
    recv_all(1, spec_tx, spec_rx)

    @pl.loop(0, chunks)
    def _(i):
        at = pl.ds(pl.multiple_of(i * step, step), step)
        lower = pl.ds(pl.multiple_of(rows + i * step, step), step)
        gain = spec_rx[pl.ds(i * 4, 4)].astype(F32)
        gain_r = gain[:, : 2 * cb].reshape(step, tok)
        gain_i = gain[:, 2 * cb :].reshape(step, tok)
        real, imag = freq[at, :tok], freq[at, tok:]
        filt = jnp.concatenate(
            [
                (real * gain_r - imag * gain_i).astype(BF),
                (real * gain_i + imag * gain_r).astype(BF),
            ],
            axis=1,
        )
        back = jnp.dot(filt, mi[...], preferred_element_type=F32)
        real, imag = back[:, :tok], back[:, tok:]
        u, w = tw[0, at, :], tw[1, at, :]
        second[at, :] = (real * u - imag * w).astype(BF)
        second[lower, :] = (imag * u + real * w).astype(BF)

    scale = 1.0 / (2 * n * tok)
    out_step = 4 * cb
    out_groups = n // 4

    @pl.loop(0, out_groups)
    def _(s):
        i = lax.rem(me // 4 + 1 + s, out_groups)
        at = pl.ds(pl.multiple_of(i * out_step, out_step), out_step)
        conv = jnp.dot(wi[at, :], second[...], preferred_element_type=F32) * scale
        conv_tx[pl.ds(i * 4, 4)] = conv.astype(BF).reshape(4, cb, tok)

        @pl.loop(0, 4)
        def _(r):
            dest = i * 4 + r

            @pl.when(dest != me)
            def _():
                exchange(2, conv_tx, conv_rx, dest).start()

    conv_rx[pl.ds(me, 1)] = conv_tx[pl.ds(me, 1)]
    middle = min(early + MIDDLE, last_step)
    for d in range(early + 1, middle + 1):
        ring_step(d)
    recv_all(2, conv_tx, conv_rx)

    def gated_half(g):
        parts = []
        for block in range(2):
            at = pl.ds(g * (n // 4) + block * (n // 2), n // 4)
            conv = conv_rx[at].reshape(chan // 4, tok).astype(F32)
            gate = gate_t[at].reshape(chan // 4, tok).astype(F32)
            parts.append((conv * gate).astype(BF))
        return jnp.concatenate(parts, axis=0).T

    feat_tx[...] = gated_half(1 - half)
    hand = pltpu.make_async_remote_copy(
        src_ref=feat_tx,
        dst_ref=feats.at[1, mine],
        send_sem=pair_sem.at[1],
        recv_sem=f_recv.at[1, mine],
        device_id={"ctx": partner},
        device_id_type=MESH,
    )
    hand.start()
    feats[0, pl.ds(mine, 1)] = gated_half(half)[None]

    def feat_copy(route, w, owner):
        dest = group_at(*((0, 1, 0), (1, 0, 0), (-1, 0, 0), (0, 0, 1))[route])
        return pltpu.make_async_remote_copy(
            src_ref=feats.at[w, owner],
            dst_ref=feats.at[w, owner],
            send_sem=f_send.at[route, w, owner],
            recv_sem=f_recv.at[w, owner],
            device_id={"tp": dest},
            device_id_type=MESH,
        )

    sent = []
    order = [(0, 0)]
    if Y_LOW > 1:
        order.append((0, 1))
    if x_count > 1:
        order += [(dx, dy) for dy in range(Y_LOW) for dx in (-1, 1)]
        order += [(2, dy) for dy in range(Y_LOW)]
    d = middle + 1
    for i, (dx, dy) in enumerate(order):
        for w in range(2):
            owner = group_at(dx, dy, 0)
            routes = []
            if i == 0 and Y_LOW > 1:
                routes.append(0)
            if dx == 0 and x_count > 1:
                routes += [1, 2]
            if dx == -1 and (w + dy) % 2 == 0:
                routes.append(1)
            if dx == 1 and (w + dy) % 2 == 1:
                routes.append(2)
            if CORES > 1:
                routes.append(3)
            if i > 0 or w > 0:
                feat_copy(0, w, owner).wait_recv()
            for route in routes:
                copy = feat_copy(route, w, owner)
                copy.start()
                sent.append(copy)
        if d <= last_step:
            ring_step(d)
            d += 1
    for d in range(d, last_step + 1):
        ring_step(d)
    if CORES > 1:
        for dx, dy in order:
            for w in range(2):
                feat_copy(0, w, group_at(dx, dy, 1)).wait_recv()

    def product(w):
        left = jnp.concatenate([feats[w, t] for t in range(groups)], axis=1)
        return jnp.dot(
            left, weights[...].reshape(n * half_rows, chan), preferred_element_type=F32
        )

    part_tx[...] = product(1).astype(BF)
    swap = pltpu.make_async_remote_copy(
        src_ref=part_tx,
        dst_ref=part_rx,
        send_sem=pair_sem.at[2],
        recv_sem=pair_sem.at[3],
        device_id={"ctx": partner},
        device_id_type=MESH,
    )
    swap.start()
    total = product(0)
    swap.wait_recv()
    out_ref[...] = (total + part_rx[...].astype(F32)).astype(BF)

    drain(0, sig_tx, sig_rx)
    drain(1, spec_tx, spec_rx)
    drain(2, conv_tx, conv_rx)
    for way in range(2):
        for kind in range(2):
            for d in range(reach(kind, way)):
                ring_copy(kind, way, d).wait_send()
    for copy in sent:
        copy.wait_send()
    lend.wait_send()
    hand.wait_send()
    swap.wait_send()


def local(query_branch, value_branch, gate_branch, spectrum_real, spectrum_imag, projection):
    n, groups = lax.axis_size("ctx"), lax.axis_size("tp")
    tok, chan = query_branch.shape
    cb = chan // n
    rows = 2 * n * cb
    half_rows = projection.shape[0] // 2
    consts = [jnp.asarray(t) for t in tables(n, tok, cb)]
    inputs = (query_branch, value_branch, gate_branch, spectrum_real, spectrum_imag)
    dma = pltpu.SemaphoreType.DMA
    return pl.pallas_call(
        functools.partial(layer_kernel, n, groups),
        out_shape=jax.ShapeDtypeStruct((tok, chan), BF),
        in_specs=[pl.BlockSpec(memory_space=pl.ANY)] * 11,
        out_specs=pl.BlockSpec(memory_space=pltpu.VMEM),
        scratch_shapes=[pltpu.VMEM(t.shape, t.dtype) for t in inputs]
        + [pltpu.VMEM(t.shape, t.dtype) for t in consts]
        + [
            pltpu.VMEM((n, cb, tok), BF),
            pltpu.VMEM((n, cb, tok), BF),
            pltpu.VMEM((n, 4 * cb, tok), BF),
            pltpu.VMEM((n, 4 * cb, tok), BF),
            pltpu.VMEM((rows, 2 * tok), F32),
            pltpu.VMEM((2 * rows, tok), BF),
            pltpu.VMEM((n, cb, tok), BF),
            pltpu.VMEM((n, cb, tok), BF),
            pltpu.VMEM((n, cb, tok), BF),
            pltpu.VMEM((n, half_rows, chan), BF),
            pltpu.VMEM((tok, chan // 2), BF),
            pltpu.VMEM((2, groups, tok, chan // 2), BF),
            pltpu.VMEM((tok, chan), BF),
            pltpu.VMEM((tok, chan), BF),
            dma((11,)),
            dma((3, n)),
            dma((3, n)),
            dma((2, n)),
            dma((n,)),
            dma((4, 2, groups)),
            dma((2, groups)),
            dma((4,)),
        ],
        compiler_params=pltpu.CompilerParams(
            collective_id=0, has_side_effects=True, vmem_limit_bytes=60 << 20
        ),
        cost_estimate=pl.CostEstimate(
            flops=4 * 10**9, bytes_accessed=10 << 20, transcendentals=0
        ),
    )(*inputs, projection, *consts)


def solution(mesh):
    return jax.shard_map(
        local,
        mesh=mesh,
        in_specs=(
            P("ctx", "tp"),
            P("ctx", "tp"),
            P("ctx", "tp"),
            P("ctx", None, "tp"),
            P("ctx", None, "tp"),
            P("ctx", "tp"),
        ),
        out_specs=P("ctx", "tp"),
        check_vma=False,
    )
```

```python
import functools
import math

import jax
import jax.numpy as jnp
import ml_dtypes
import numpy as np
from jax import lax
from jax.experimental import pallas as pl
from jax.experimental.pallas import tpu as pltpu
from jax.sharding import PartitionSpec as P

MESH = pl.DeviceIdType.MESH
BF = jnp.bfloat16
F32 = jnp.float32
Y_LOW = 2
CORES = 2
ROUNDS = 1


def cos_sin(grid, period):
    angles = grid.astype(np.float32) * np.float32(2.0 * math.pi / period)
    return np.cos(angles), np.sin(angles)


def tables(n, tok, cb):
    outer = 2 * n
    k, p, j = np.arange(outer), np.arange(n), np.arange(tok)
    bf = ml_dtypes.bfloat16
    co, so = (t.astype(bf).astype(np.float32) for t in cos_sin(k[:, None] * p[None, :], outer))
    ci, si = (t.astype(bf).astype(np.float32) for t in cos_sin(j[:, None] * j[None, :] % tok, tok))
    eye = np.eye(cb, dtype=np.float32)
    outer_fwd = np.concatenate([np.kron(co, eye), -np.kron(so, eye)], 0).astype(bf)
    outer_inv = np.ascontiguousarray(outer_fwd.T)
    inner_fwd = np.block([[ci, -si], [si, ci]]).astype(bf)
    inner_inv = np.block([[ci, si], [-si, ci]]).astype(bf)
    twid = np.stack([np.repeat(t, cb, 0) for t in cos_sin(k[:, None] * j[None, :], outer * tok)])
    return outer_fwd, outer_inv, inner_fwd, inner_inv, twid.astype(np.float32)


def peer(step, me, n):
    z_count = n // 2
    half, z = me // z_count, lax.rem(me, z_count)
    flip, u = lax.rem(step, 2), step // 2
    shift = jnp.where(lax.rem(u, 2) == 1, (u + 1) // 2, z_count - u // 2)
    return lax.rem(half + flip, 2) * z_count + lax.rem(z + shift, z_count)


def layer_kernel(
    n,
    groups,
    q_hbm,
    v_hbm,
    gate_hbm,
    sr_hbm,
    si_hbm,
    proj_hbm,
    wf_hbm,
    wi_hbm,
    mf_hbm,
    mi_hbm,
    tw_hbm,
    out_ref,
    q_ref,
    v_ref,
    gate_ref,
    sr_ref,
    si_ref,
    wf,
    wi,
    mf,
    mi,
    tw,
    sig_tx,
    sig_rx,
    spec_tx,
    spec_rx,
    freq,
    second,
    conv_tx,
    conv_rx,
    weights,
    feat_tx,
    feats,
    part_tx,
    part_rx,
    load_sem,
    send_sem,
    recv_sem,
    w_send,
    w_recv,
    f_send,
    f_recv,
    pair_sem,
    hand_sem,
    c_recv,
):
    me = lax.axis_index("ctx")
    mine = lax.axis_index("tp")
    tok, chan = q_ref.shape
    cb = chan // n
    sub = cb // ROUNDS
    rows = 2 * n * sub
    z_count = n // 2
    half, z = me // z_count, lax.rem(me, z_count)
    partner = (1 - half) * z_count + z
    x_count = groups // (Y_LOW * CORES)
    core = lax.rem(mine, CORES)
    y_low = lax.rem(mine // CORES, Y_LOW)
    x = mine // (CORES * Y_LOW)
    half_rows = proj_hbm.shape[0] // 2

    def group_at(dx, dy, dc):
        return (
            lax.rem(x + dx + x_count, x_count) * Y_LOW + lax.rem(y_low + dy, Y_LOW)
        ) * CORES + lax.rem(core + dc, CORES)

    near = []
    if x_count > 1:
        near += [group_at(1, 0, 0), group_at(-1, 0, 0)]
    if Y_LOW > 1:
        near.append(group_at(0, 1, 0))
    if CORES > 1:
        near.append(group_at(0, 0, 1))

    barrier = pltpu.get_barrier_semaphore()

    @pl.loop(1, n)
    def _(s):
        pl.semaphore_signal(barrier, inc=1, device_id={"ctx": peer(s, me, n)}, device_id_type=MESH)

    for other in near:
        pl.semaphore_signal(barrier, inc=1, device_id={"tp": other}, device_id_type=MESH)

    pairs = (
        (q_hbm, q_ref),
        (v_hbm, v_ref),
        (proj_hbm.at[pl.ds(pl.multiple_of(half * half_rows, half_rows), half_rows)], weights.at[lax.rem(me, ROUNDS), me // ROUNDS]),
        (sr_hbm, sr_ref),
        (si_hbm, si_ref),
        (gate_hbm, gate_ref),
        (wf_hbm, wf),
        (tw_hbm, tw),
        (mf_hbm, mf),
        (mi_hbm, mi),
        (wi_hbm, wi),
    )
    loads = [pltpu.make_async_copy(a, b, load_sem.at[i]) for i, (a, b) in enumerate(pairs)]
    for load in loads:
        load.start()

    def exchange(kind, tx, rx, dest):
        return pltpu.make_async_remote_copy(
            src_ref=tx.at[dest],
            dst_ref=rx.at[me],
            send_sem=send_sem.at[kind],
            recv_sem=recv_sem.at[kind],
            device_id={"ctx": dest},
            device_id_type=MESH,
        )

    def send_all(kind, tx, rx):
        @pl.loop(1, n)
        def _(s):
            exchange(kind, tx, rx, peer(s, me, n)).start()

    def whole(ref, sem):
        return pltpu.make_async_copy(ref, ref, sem)

    def recv_all(kind, tx, rx):
        whole(rx.at[pl.ds(0, n - 1)], recv_sem.at[kind]).wait()

    def drain(kind, tx, rx):
        whole(tx.at[pl.ds(0, n - 1)], send_sem.at[kind]).wait()

    def reach(kind, way):
        return z_count // 2 - (kind + way) % 2

    def ring_copy(kind, way, d):
        sign = 1 - 2 * way
        owner = (half if kind == 0 else 1 - half) * z_count + lax.rem(
            z - sign * d + z_count, z_count
        )
        dest = half * z_count + lax.rem(z + sign + z_count, z_count)
        return pltpu.make_async_remote_copy(
            src_ref=weights.at[lax.rem(owner, ROUNDS), owner // ROUNDS],
            dst_ref=weights.at[lax.rem(owner, ROUNDS), owner // ROUNDS],
            send_sem=w_send.at[way],
            recv_sem=w_recv.at[owner],
            device_id={"ctx": dest},
            device_id_type=MESH,
        )

    def ring_step(d, kind):
        if d == 0 and kind == 0:
            loads[2].wait()
        if d == 0 and kind == 1:
            ring_copy(1, 0, 0).wait_recv()
        for way in range(2):
            if 1 <= d <= reach(kind, way):
                ring_copy(kind, way, d).wait_recv()
            if d < reach(kind, way):
                ring_copy(kind, way, d).start()

    ring_todo = [(d, kind) for d in range(z_count // 2 + 1) for kind in range(2)]
    lend = pltpu.make_async_remote_copy(
        src_ref=proj_hbm.at[pl.ds(pl.multiple_of((1 - half) * half_rows, half_rows), half_rows)],
        dst_ref=weights.at[lax.rem(me, ROUNDS), me // ROUNDS],
        send_sem=pair_sem.at[0],
        recv_sem=w_recv.at[me],
        device_id={"ctx": partner},
        device_id_type=MESH,
    )

    def ring(count):
        for _ in range(min(count, len(ring_todo))):
            ring_step(*ring_todo.pop(0))

    def by_owner(values):
        return values.T.reshape(n, sub, tok)

    def spec_turn(r):
        cols = slice(r * n * sub, (r + 1) * n * sub)
        for part, ref in enumerate((sr_ref, si_ref)):
            both = [by_owner(ref[k, :, cols].astype(F32)) for k in range(2)]
            at = 2 * part * sub
            spec_tx[r, :, at : at + 2 * sub, :] = jnp.concatenate(both, axis=1).astype(BF)
        spec_rx[r, pl.ds(me, 1)] = spec_tx[r, pl.ds(me, 1)]

    def spec_send(r):
        send_all(1 + r, spec_tx.at[r], spec_rx.at[r])

    loads[0].wait()
    loads[1].wait()
    signal = q_ref[...].astype(F32) * v_ref[...].astype(F32)
    sig_tx[...] = jnp.concatenate(
        [by_owner(signal[:, r * n * sub : (r + 1) * n * sub]) for r in range(ROUNDS)], axis=1
    ).astype(BF)
    pl.semaphore_wait(barrier, n - 1 + len(near))
    send_all(0, sig_tx, sig_rx)
    lend.start()
    step = 16 * sub
    chunks = rows // step

    def forward():
        recv_all(0, sig_tx, sig_rx)
        drain(0, sig_tx, sig_rx)
        sig_rx[pl.ds(me, 1)] = sig_tx[pl.ds(me, 1)]
        for load in loads[5:]:
            load.wait()
        for r in range(ROUNDS):
            block = sig_rx[...].astype(F32)[:, r * sub : (r + 1) * sub]
            second[: n * sub, :] = block.reshape(n * sub, tok).astype(BF)

            @pl.loop(0, chunks)
            def _(i):
                at = pl.ds(pl.multiple_of(i * step, step), step)
                lower = pl.ds(pl.multiple_of(rows + i * step, step), step)
                grid = second[: n * sub, :]
                real = jnp.dot(wf[at, :], grid, preferred_element_type=F32)
                imag = jnp.dot(wf[lower, :], grid, preferred_element_type=F32)
                u, w = tw[0, at, :], tw[1, at, :]
                first = jnp.concatenate(
                    [(real * u + imag * w).astype(BF), (imag * u - real * w).astype(BF)], axis=1
                )
                freq[r, at, :] = jnp.dot(first, mf[...], preferred_element_type=F32)

    scale = 1.0 / (2 * n * tok)
    side = tok // ROUNDS

    def filter_round(r):
        recv_all(1 + r, spec_tx.at[r], spec_rx.at[r])

        @pl.loop(0, chunks)
        def _(i):
            at = pl.ds(pl.multiple_of(i * step, step), step)
            lower = pl.ds(pl.multiple_of(rows + i * step, step), step)
            gain = spec_rx[r, pl.ds(i * 8, 8)].astype(F32)
            gain_r = gain[:, : 2 * sub].reshape(step, tok)
            gain_i = gain[:, 2 * sub :].reshape(step, tok)
            real, imag = freq[r, at, :tok], freq[r, at, tok:]
            filt = jnp.concatenate(
                [
                    (real * gain_r - imag * gain_i).astype(BF),
                    (real * gain_i + imag * gain_r).astype(BF),
                ],
                axis=1,
            )
            back = jnp.dot(filt, mi[...], preferred_element_type=F32)
            real, imag = back[:, :tok], back[:, tok:]
            u, w = tw[0, at, :], tw[1, at, :]
            second[at, :] = (real * u - imag * w).astype(BF)
            second[lower, :] = (imag * u + real * w).astype(BF)

        conv = jnp.dot(wi[...], second[...], preferred_element_type=F32) * scale
        conv = conv.reshape(n, sub, tok)
        conv_tx[r] = jnp.concatenate(
            [conv[:, :, i * side : (i + 1) * side] for i in range(ROUNDS)], axis=1
        ).astype(BF)
        send_all(1 + ROUNDS + r, conv_tx.at[r], conv_rx.at[r])
        conv_rx[r, pl.ds(me, 1)] = conv_tx[r, pl.ds(me, 1)]

    quarter = chan // 4
    blocks = 2 // ROUNDS
    hands = []

    def gated_half(r, g):
        parts = []
        for i in range(blocks):
            first = i * 2 * quarter + g * quarter
            conv = conv_rx[r, pl.ds(first // sub, quarter // sub)].astype(F32)
            cols = pl.ds(pl.multiple_of(r * 2 * quarter + first, quarter), quarter)
            gated = []
            for p in range(ROUNDS):
                turned = conv[:, p * sub : (p + 1) * sub].reshape(quarter, side).T
                gate = gate_ref[p * side : (p + 1) * side, cols].astype(F32)
                gated.append((turned * gate).astype(BF))
            parts.append(jnp.concatenate(gated, axis=0))
        return jnp.concatenate(parts, axis=1)

    def feat_copy(route, w, r, owner):
        dest = group_at(*((0, 1, 0), (1, 0, 0), (-1, 0, 0), (0, 0, 1))[route])
        return pltpu.make_async_remote_copy(
            src_ref=feats.at[w, r, owner],
            dst_ref=feats.at[w, r, owner],
            send_sem=f_send.at[r],
            recv_sem=c_recv.at[r] if route == 3 else f_recv.at[w, r, owner],
            device_id={"tp": dest},
            device_id_type=MESH,
        )

    sent = [0] * ROUNDS
    order = [(0, 0)]
    if Y_LOW > 1:
        order.append((0, 1))
    if x_count > 1:
        order += [(dx, dy) for dy in range(Y_LOW) for dx in (-1, 1)]
        order += [(2, dy) for dy in range(Y_LOW)]
    todo = [[(i, w) for i in range(len(order)) for w in range(2)] for _ in range(ROUNDS)]

    def relay(r, i, w):
        dx, dy = order[i]
        owner = group_at(dx, dy, 0)
        routes = []
        if i == 0 and Y_LOW > 1:
            routes.append(0)
        if dx == 0 and x_count > 1:
            routes += [1, 2]
        if dx == -1 and (w + dy) % 2 == 0:
            routes.append(1)
        if dx == 1 and (w + dy) % 2 == 1:
            routes.append(2)
        if CORES > 1:
            routes.append(3)
        if i > 0 or w > 0:
            feat_copy(0, w, r, owner).wait_recv()
        for route in routes:
            feat_copy(route, w, r, owner).start()
            sent[r] += 1

    def relays(r, count):
        for _ in range(min(count, len(todo[r]))):
            relay(r, *todo[r].pop(0))

    def features(r):
        recv_all(1 + ROUNDS + r, conv_tx.at[r], conv_rx.at[r])
        feat_tx[r] = gated_half(r, 1 - half)
        hand = pltpu.make_async_remote_copy(
            src_ref=feat_tx.at[r],
            dst_ref=feats.at[1, r, mine],
            send_sem=hand_sem.at[r],
            recv_sem=f_recv.at[1, r, mine],
            device_id={"ctx": partner},
            device_id_type=MESH,
        )
        hand.start()
        hands.append(hand)
        feats[0, r, pl.ds(mine, 1)] = gated_half(r, half)[None]
        relays(r, 1)

    loads[3].wait()
    loads[4].wait()
    spec_turn(0)
    spec_send(0)
    forward()
    ring(4)
    filter_round(0)
    drain(1, spec_tx.at[0], spec_rx.at[0])
    ring(4)
    features(0)
    ring(2)
    relays(0, 2)
    ring(1)
    relays(0, 2)
    ring(1)
    relays(0, 2)
    ring(1)
    relays(0, 2)
    ring(1)
    relays(0, 2)
    ring(1)
    relays(0, 2)
    ring(1)
    relays(0, 2)
    ring(1)
    relays(0, 2)
    ring(1)
    relays(0, 2)
    ring(1)
    relays(0, 2)
    relays(0, 99)
    ring(99)
    if CORES > 1:
        for r in range(ROUNDS):
            whole(feats.at[:, r, pl.ds(0, groups // 2)], c_recv.at[r]).wait()

    def product(w):
        parts = []
        for r in range(ROUNDS):
            left = jnp.concatenate([feats[w, r, t] for t in range(groups)], axis=1)
            right = weights[r].reshape(n // ROUNDS * half_rows, chan)
            parts.append(jnp.dot(left, right, preferred_element_type=F32))
        return sum(parts)

    part_tx[...] = product(1).astype(BF)
    swap = pltpu.make_async_remote_copy(
        src_ref=part_tx,
        dst_ref=part_rx,
        send_sem=pair_sem.at[1],
        recv_sem=pair_sem.at[2],
        device_id={"ctx": partner},
        device_id_type=MESH,
    )
    swap.start()
    total = product(0)
    swap.wait_recv()
    out_ref[...] = (total + part_rx[...].astype(F32)).astype(BF)

    for r in range(ROUNDS):
        drain(1 + ROUNDS + r, conv_tx.at[r], conv_rx.at[r])
    for way in range(2):
        whole(weights.at[0, pl.ds(0, z_count - 1)], w_send.at[way]).wait()
    for r in range(ROUNDS):
        whole(feats.at[:, r, pl.ds(0, sent[r] // 2)], f_send.at[r]).wait()
    lend.wait_send()
    for hand in hands:
        hand.wait_send()
    swap.wait_send()


def local(query_branch, value_branch, gate_branch, spectrum_real, spectrum_imag, projection):
    n, groups = lax.axis_size("ctx"), lax.axis_size("tp")
    tok, chan = query_branch.shape
    cb = chan // n
    sub = cb // ROUNDS
    rows = 2 * n * sub
    half_rows = projection.shape[0] // 2
    consts = [jnp.asarray(t) for t in tables(n, tok, sub)]
    inputs = (query_branch, value_branch, gate_branch, spectrum_real, spectrum_imag)
    dma = pltpu.SemaphoreType.DMA
    return pl.pallas_call(
        functools.partial(layer_kernel, n, groups),
        out_shape=jax.ShapeDtypeStruct((tok, chan), BF),
        in_specs=[pl.BlockSpec(memory_space=pl.ANY)] * 11,
        out_specs=pl.BlockSpec(memory_space=pltpu.VMEM),
        scratch_shapes=[pltpu.VMEM(t.shape, t.dtype) for t in inputs]
        + [pltpu.VMEM(t.shape, t.dtype) for t in consts]
        + [
            pltpu.VMEM((n, cb, tok), BF),
            pltpu.VMEM((n, cb, tok), BF),
            pltpu.VMEM((ROUNDS, n, 4 * sub, tok), BF),
            pltpu.VMEM((ROUNDS, n, 4 * sub, tok), BF),
            pltpu.VMEM((ROUNDS, rows, 2 * tok), F32),
            pltpu.VMEM((2 * rows, tok), BF),
            pltpu.VMEM((ROUNDS, n, cb, tok // ROUNDS), BF),
            pltpu.VMEM((ROUNDS, n, cb, tok // ROUNDS), BF),
            pltpu.VMEM((ROUNDS, n // ROUNDS, half_rows, chan), BF),
            pltpu.VMEM((ROUNDS, tok, chan // 2 // ROUNDS), BF),
            pltpu.VMEM((2, ROUNDS, groups, tok, chan // 2 // ROUNDS), BF),
            pltpu.VMEM((tok, chan), BF),
            pltpu.VMEM((tok, chan), BF),
            dma((11,)),
            dma((1 + 2 * ROUNDS,)),
            dma((1 + 2 * ROUNDS,)),
            dma((2,)),
            dma((n,)),
            dma((ROUNDS,)),
            dma((2, ROUNDS, groups)),
            dma((3,)),
            dma((ROUNDS,)),
            dma((ROUNDS,)),
        ],
        compiler_params=pltpu.CompilerParams(
            collective_id=0, has_side_effects=True, vmem_limit_bytes=60 << 20
        ),
        cost_estimate=pl.CostEstimate(
            flops=4 * 10**9, bytes_accessed=10 << 20, transcendentals=0
        ),
    )(*inputs, projection, *consts)


def solution(mesh):
    return jax.shard_map(
        local,
        mesh=mesh,
        in_specs=(
            P("ctx", "tp"),
            P("ctx", "tp"),
            P("ctx", "tp"),
            P("ctx", None, "tp"),
            P("ctx", None, "tp"),
            P("ctx", "tp"),
        ),
        out_specs=P("ctx", "tp"),
        check_vma=False,
    )
```

```python
import functools
import math

import jax
import jax.numpy as jnp
import ml_dtypes
import numpy as np
from jax import lax
from jax.experimental import pallas as pl
from jax.experimental.pallas import tpu as pltpu
from jax.sharding import PartitionSpec as P

MESH = pl.DeviceIdType.MESH
BF = jnp.bfloat16
F32 = jnp.float32
Y_LOW = 2
CORES = 2
ROUNDS = 1


def cos_sin(grid, period):
    angles = grid.astype(np.float32) * np.float32(2.0 * math.pi / period)
    return np.cos(angles), np.sin(angles)


def tables(n, tok, cb):
    outer = 2 * n
    k, p, j = np.arange(outer), np.arange(n), np.arange(tok)
    bf = ml_dtypes.bfloat16
    co, so = (t.astype(bf).astype(np.float32) for t in cos_sin(k[:, None] * p[None, :], outer))
    ci, si = (t.astype(bf).astype(np.float32) for t in cos_sin(j[:, None] * j[None, :] % tok, tok))
    eye = np.eye(cb, dtype=np.float32)
    outer_fwd = np.concatenate([np.kron(co, eye), -np.kron(so, eye)], 0).astype(bf)
    outer_inv = np.ascontiguousarray(outer_fwd.T)
    inner_fwd = np.block([[ci, -si], [si, ci]]).astype(bf)
    inner_inv = np.block([[ci, si], [-si, ci]]).astype(bf)
    twid = np.stack([np.repeat(t, cb, 0) for t in cos_sin(k[:, None] * j[None, :], outer * tok)])
    return outer_fwd, outer_inv, inner_fwd, inner_inv, twid.astype(np.float32)


def peer(step, me, n):
    z_count = n // 2
    half, z = me // z_count, lax.rem(me, z_count)
    flip, u = lax.rem(step, 2), step // 2
    shift = jnp.where(lax.rem(u, 2) == 1, (u + 1) // 2, z_count - u // 2)
    return lax.rem(half + flip, 2) * z_count + lax.rem(z + shift, z_count)


def layer_kernel(
    n,
    groups,
    q_hbm,
    v_hbm,
    gate_hbm,
    sr_hbm,
    si_hbm,
    proj_hbm,
    wf_hbm,
    wi_hbm,
    mf_hbm,
    mi_hbm,
    tw_hbm,
    out_ref,
    q_ref,
    v_ref,
    gate_ref,
    sr_ref,
    si_ref,
    wf,
    wi,
    mf,
    mi,
    tw,
    sig_tx,
    sig_rx,
    spec_tx,
    spec_rx,
    freq,
    second,
    conv_tx,
    conv_rx,
    weights,
    feat_tx,
    feats,
    part_tx,
    part_rx,
    load_sem,
    send_sem,
    recv_sem,
    w_send,
    w_recv,
    f_send,
    f_recv,
    pair_sem,
    hand_sem,
    c_recv,
):
    me = lax.axis_index("ctx")
    mine = lax.axis_index("tp")
    tok, chan = q_ref.shape
    cb = chan // n
    sub = cb // ROUNDS
    rows = 2 * n * sub
    z_count = n // 2
    half, z = me // z_count, lax.rem(me, z_count)
    partner = (1 - half) * z_count + z
    x_count = groups // (Y_LOW * CORES)
    core = lax.rem(mine, CORES)
    y_low = lax.rem(mine // CORES, Y_LOW)
    x = mine // (CORES * Y_LOW)
    half_rows = proj_hbm.shape[0] // 2

    def group_at(dx, dy, dc):
        return (
            lax.rem(x + dx + x_count, x_count) * Y_LOW + lax.rem(y_low + dy, Y_LOW)
        ) * CORES + lax.rem(core + dc, CORES)

    near = []
    if x_count > 1:
        near += [group_at(1, 0, 0), group_at(-1, 0, 0)]
    if Y_LOW > 1:
        near.append(group_at(0, 1, 0))
    if CORES > 1:
        near.append(group_at(0, 0, 1))

    barrier = pltpu.get_barrier_semaphore()

    @pl.loop(1, n)
    def _(s):
        pl.semaphore_signal(barrier, inc=1, device_id={"ctx": peer(s, me, n)}, device_id_type=MESH)

    for other in near:
        pl.semaphore_signal(barrier, inc=1, device_id={"tp": other}, device_id_type=MESH)

    pairs = (
        (q_hbm, q_ref),
        (v_hbm, v_ref),
        (proj_hbm.at[pl.ds(pl.multiple_of(half * half_rows, half_rows), half_rows)], weights.at[lax.rem(me, ROUNDS), me // ROUNDS]),
        (sr_hbm, sr_ref),
        (si_hbm, si_ref),
        (gate_hbm, gate_ref),
        (wf_hbm, wf),
        (tw_hbm, tw),
        (mf_hbm, mf),
        (mi_hbm, mi),
        (wi_hbm, wi),
    )
    loads = [pltpu.make_async_copy(a, b, load_sem.at[i]) for i, (a, b) in enumerate(pairs)]
    for load in loads:
        load.start()

    def exchange(kind, tx, rx, dest):
        return pltpu.make_async_remote_copy(
            src_ref=tx.at[dest],
            dst_ref=rx.at[me],
            send_sem=send_sem.at[kind],
            recv_sem=recv_sem.at[kind],
            device_id={"ctx": dest},
            device_id_type=MESH,
        )

    def send_all(kind, tx, rx):
        @pl.loop(1, n)
        def _(s):
            exchange(kind, tx, rx, peer(s, me, n)).start()

    def whole(ref, sem):
        return pltpu.make_async_copy(ref, ref, sem)

    def recv_all(kind, tx, rx):
        whole(rx.at[pl.ds(0, n - 1)], recv_sem.at[kind]).wait()

    def drain(kind, tx, rx):
        whole(tx.at[pl.ds(0, n - 1)], send_sem.at[kind]).wait()

    def reach(kind, way):
        return z_count // 2 - (kind + way) % 2

    def ring_copy(kind, way, d):
        sign = 1 - 2 * way
        owner = (half if kind == 0 else 1 - half) * z_count + lax.rem(
            z - sign * d + z_count, z_count
        )
        dest = half * z_count + lax.rem(z + sign + z_count, z_count)
        return pltpu.make_async_remote_copy(
            src_ref=weights.at[lax.rem(owner, ROUNDS), owner // ROUNDS],
            dst_ref=weights.at[lax.rem(owner, ROUNDS), owner // ROUNDS],
            send_sem=w_send.at[way],
            recv_sem=w_recv.at[owner],
            device_id={"ctx": dest},
            device_id_type=MESH,
        )

    def ring_step(d, kind):
        if d == 0 and kind == 0:
            loads[2].wait()
        if d == 0 and kind == 1:
            ring_copy(1, 0, 0).wait_recv()
        for way in range(2):
            if 1 <= d <= reach(kind, way):
                ring_copy(kind, way, d).wait_recv()
            if d < reach(kind, way):
                ring_copy(kind, way, d).start()

    ring_todo = [(d, kind) for d in range(z_count // 2 + 1) for kind in range(2)]
    lend = pltpu.make_async_remote_copy(
        src_ref=proj_hbm.at[pl.ds(pl.multiple_of((1 - half) * half_rows, half_rows), half_rows)],
        dst_ref=weights.at[lax.rem(me, ROUNDS), me // ROUNDS],
        send_sem=pair_sem.at[0],
        recv_sem=w_recv.at[me],
        device_id={"ctx": partner},
        device_id_type=MESH,
    )

    def ring(count):
        for _ in range(min(count, len(ring_todo))):
            ring_step(*ring_todo.pop(0))

    def by_owner(values):
        return values.T.reshape(n, sub, tok)

    def spec_turn(r):
        cols = slice(r * n * sub, (r + 1) * n * sub)
        for part, ref in enumerate((sr_ref, si_ref)):
            both = [by_owner(ref[k, :, cols].astype(F32)) for k in range(2)]
            at = 2 * part * sub
            spec_tx[r, :, at : at + 2 * sub, :] = jnp.concatenate(both, axis=1).astype(BF)
        spec_rx[r, pl.ds(me, 1)] = spec_tx[r, pl.ds(me, 1)]

    def spec_send(r):
        send_all(1 + r, spec_tx.at[r], spec_rx.at[r])

    loads[0].wait()
    loads[1].wait()
    signal = q_ref[...].astype(F32) * v_ref[...].astype(F32)
    sig_tx[...] = jnp.concatenate(
        [by_owner(signal[:, r * n * sub : (r + 1) * n * sub]) for r in range(ROUNDS)], axis=1
    ).astype(BF)
    pl.semaphore_wait(barrier, n - 1 + len(near))
    send_all(0, sig_tx, sig_rx)
    lend.start()
    step = 16 * sub
    chunks = rows // step

    def forward():
        recv_all(0, sig_tx, sig_rx)
        drain(0, sig_tx, sig_rx)
        sig_rx[pl.ds(me, 1)] = sig_tx[pl.ds(me, 1)]
        for load in loads[5:]:
            load.wait()
        for r in range(ROUNDS):
            block = sig_rx[...].astype(F32)[:, r * sub : (r + 1) * sub]
            second[: n * sub, :] = block.reshape(n * sub, tok).astype(BF)

            @pl.loop(0, chunks)
            def _(i):
                at = pl.ds(pl.multiple_of(i * step, step), step)
                lower = pl.ds(pl.multiple_of(rows + i * step, step), step)
                grid = second[: n * sub, :]
                real = jnp.dot(wf[at, :], grid, preferred_element_type=F32)
                imag = jnp.dot(wf[lower, :], grid, preferred_element_type=F32)
                u, w = tw[0, at, :], tw[1, at, :]
                first = jnp.concatenate(
                    [(real * u + imag * w).astype(BF), (imag * u - real * w).astype(BF)], axis=1
                )
                freq[r, at, :] = jnp.dot(first, mf[...], preferred_element_type=F32)

    scale = 1.0 / (2 * n * tok)
    side = tok // ROUNDS

    def filter_round(r):
        recv_all(1 + r, spec_tx.at[r], spec_rx.at[r])

        @pl.loop(0, chunks)
        def _(i):
            at = pl.ds(pl.multiple_of(i * step, step), step)
            lower = pl.ds(pl.multiple_of(rows + i * step, step), step)
            gain = spec_rx[r, pl.ds(i * 8, 8)].astype(F32)
            gain_r = gain[:, : 2 * sub].reshape(step, tok)
            gain_i = gain[:, 2 * sub :].reshape(step, tok)
            real, imag = freq[r, at, :tok], freq[r, at, tok:]
            filt = jnp.concatenate(
                [
                    (real * gain_r - imag * gain_i).astype(BF),
                    (real * gain_i + imag * gain_r).astype(BF),
                ],
                axis=1,
            )
            back = jnp.dot(filt, mi[...], preferred_element_type=F32)
            real, imag = back[:, :tok], back[:, tok:]
            u, w = tw[0, at, :], tw[1, at, :]
            second[at, :] = (real * u - imag * w).astype(BF)
            second[lower, :] = (imag * u + real * w).astype(BF)

        conv = jnp.dot(wi[...], second[...], preferred_element_type=F32) * scale
        conv = conv.reshape(n, sub, tok)
        conv_tx[r] = jnp.concatenate(
            [conv[:, :, i * side : (i + 1) * side] for i in range(ROUNDS)], axis=1
        ).astype(BF)
        send_all(1 + ROUNDS + r, conv_tx.at[r], conv_rx.at[r])
        conv_rx[r, pl.ds(me, 1)] = conv_tx[r, pl.ds(me, 1)]

    quarter = chan // 4
    blocks = 2 // ROUNDS
    hands = []

    def gated_half(r, g):
        parts = []
        for i in range(blocks):
            first = i * 2 * quarter + g * quarter
            conv = conv_rx[r, pl.ds(first // sub, quarter // sub)].astype(F32)
            cols = pl.ds(pl.multiple_of(r * 2 * quarter + first, quarter), quarter)
            gated = []
            for p in range(ROUNDS):
                turned = conv[:, p * sub : (p + 1) * sub].reshape(quarter, side).T
                gate = gate_ref[p * side : (p + 1) * side, cols].astype(F32)
                gated.append((turned * gate).astype(BF))
            parts.append(jnp.concatenate(gated, axis=0))
        return jnp.concatenate(parts, axis=1)

    def feat_copy(route, w, r, owner):
        dest = group_at(*((0, 1, 0), (1, 0, 0), (-1, 0, 0), (0, 0, 1))[route])
        return pltpu.make_async_remote_copy(
            src_ref=feats.at[w, r, owner],
            dst_ref=feats.at[w, r, owner],
            send_sem=f_send.at[r],
            recv_sem=c_recv.at[r] if route == 3 else f_recv.at[w, r, owner],
            device_id={"tp": dest},
            device_id_type=MESH,
        )

    sent = [0] * ROUNDS
    order = [(0, 0)]
    if Y_LOW > 1:
        order.append((0, 1))
    if x_count > 1:
        order += [(dx, dy) for dy in range(Y_LOW) for dx in (-1, 1)]
        order += [(2, dy) for dy in range(Y_LOW)]
    todo = [[(i, w) for i in range(len(order)) for w in range(2)] for _ in range(ROUNDS)]

    def relay(r, i, w):
        dx, dy = order[i]
        owner = group_at(dx, dy, 0)
        routes = []
        if i == 0 and Y_LOW > 1:
            routes.append(0)
        if dx == 0 and x_count > 1:
            routes += [1, 2]
        if dx == -1 and (w + dy) % 2 == 0:
            routes.append(1)
        if dx == 1 and (w + dy) % 2 == 1:
            routes.append(2)
        if CORES > 1:
            routes.append(3)
        if i > 0 or w > 0:
            feat_copy(0, w, r, owner).wait_recv()
        for route in routes:
            feat_copy(route, w, r, owner).start()
            sent[r] += 1

    def relays(r, count):
        for _ in range(min(count, len(todo[r]))):
            relay(r, *todo[r].pop(0))

    def features(r):
        recv_all(1 + ROUNDS + r, conv_tx.at[r], conv_rx.at[r])
        feat_tx[r] = gated_half(r, 1 - half)
        hand = pltpu.make_async_remote_copy(
            src_ref=feat_tx.at[r],
            dst_ref=feats.at[1, r, mine],
            send_sem=hand_sem.at[r],
            recv_sem=f_recv.at[1, r, mine],
            device_id={"ctx": partner},
            device_id_type=MESH,
        )
        hand.start()
        hands.append(hand)
        feats[0, r, pl.ds(mine, 1)] = gated_half(r, half)[None]
        relays(r, 1)

    loads[3].wait()
    loads[4].wait()
    spec_turn(0)
    spec_send(0)
    forward()
    ring(3)
    filter_round(0)
    drain(1, spec_tx.at[0], spec_rx.at[0])
    ring(3)
    features(0)
    ring(3)
    relays(0, 2)
    ring(1)
    relays(0, 2)
    ring(1)
    relays(0, 2)
    ring(1)
    relays(0, 2)
    ring(1)
    relays(0, 2)
    ring(1)
    relays(0, 2)
    ring(1)
    relays(0, 2)
    ring(1)
    relays(0, 2)
    ring(1)
    relays(0, 99)
    ring(99)
    if CORES > 1:
        for r in range(ROUNDS):
            whole(feats.at[:, r, pl.ds(0, groups // 2)], c_recv.at[r]).wait()

    def product(w):
        parts = []
        for r in range(ROUNDS):
            left = jnp.concatenate([feats[w, r, t] for t in range(groups)], axis=1)
            right = weights[r].reshape(n // ROUNDS * half_rows, chan)
            parts.append(jnp.dot(left, right, preferred_element_type=F32))
        return sum(parts)

    part_tx[...] = product(1).astype(BF)
    swap = pltpu.make_async_remote_copy(
        src_ref=part_tx,
        dst_ref=part_rx,
        send_sem=pair_sem.at[1],
        recv_sem=pair_sem.at[2],
        device_id={"ctx": partner},
        device_id_type=MESH,
    )
    swap.start()
    total = product(0)
    swap.wait_recv()
    out_ref[...] = (total + part_rx[...].astype(F32)).astype(BF)

    for r in range(ROUNDS):
        drain(1 + ROUNDS + r, conv_tx.at[r], conv_rx.at[r])
    for way in range(2):
        whole(weights.at[0, pl.ds(0, z_count - 1)], w_send.at[way]).wait()
    for r in range(ROUNDS):
        whole(feats.at[:, r, pl.ds(0, sent[r] // 2)], f_send.at[r]).wait()
    lend.wait_send()
    for hand in hands:
        hand.wait_send()
    swap.wait_send()


def local(query_branch, value_branch, gate_branch, spectrum_real, spectrum_imag, projection):
    n, groups = lax.axis_size("ctx"), lax.axis_size("tp")
    tok, chan = query_branch.shape
    cb = chan // n
    sub = cb // ROUNDS
    rows = 2 * n * sub
    half_rows = projection.shape[0] // 2
    consts = [jnp.asarray(t) for t in tables(n, tok, sub)]
    inputs = (query_branch, value_branch, gate_branch, spectrum_real, spectrum_imag)
    dma = pltpu.SemaphoreType.DMA
    return pl.pallas_call(
        functools.partial(layer_kernel, n, groups),
        out_shape=pltpu.VMEM((tok, chan), BF),
        in_specs=[pl.BlockSpec(memory_space=pl.ANY)] * 11,
        out_specs=pl.BlockSpec(memory_space=pltpu.VMEM),
        scratch_shapes=[pltpu.VMEM(t.shape, t.dtype) for t in inputs]
        + [pltpu.VMEM(t.shape, t.dtype) for t in consts]
        + [
            pltpu.VMEM((n, cb, tok), BF),
            pltpu.VMEM((n, cb, tok), BF),
            pltpu.VMEM((ROUNDS, n, 4 * sub, tok), BF),
            pltpu.VMEM((ROUNDS, n, 4 * sub, tok), BF),
            pltpu.VMEM((ROUNDS, rows, 2 * tok), F32),
            pltpu.VMEM((2 * rows, tok), BF),
            pltpu.VMEM((ROUNDS, n, cb, tok // ROUNDS), BF),
            pltpu.VMEM((ROUNDS, n, cb, tok // ROUNDS), BF),
            pltpu.VMEM((ROUNDS, n // ROUNDS, half_rows, chan), BF),
            pltpu.VMEM((ROUNDS, tok, chan // 2 // ROUNDS), BF),
            pltpu.VMEM((2, ROUNDS, groups, tok, chan // 2 // ROUNDS), BF),
            pltpu.VMEM((tok, chan), BF),
            pltpu.VMEM((tok, chan), BF),
            dma((11,)),
            dma((1 + 2 * ROUNDS,)),
            dma((1 + 2 * ROUNDS,)),
            dma((2,)),
            dma((n,)),
            dma((ROUNDS,)),
            dma((2, ROUNDS, groups)),
            dma((3,)),
            dma((ROUNDS,)),
            dma((ROUNDS,)),
        ],
        compiler_params=pltpu.CompilerParams(
            collective_id=0, has_side_effects=True, vmem_limit_bytes=60 << 20
        ),
        cost_estimate=pl.CostEstimate(
            flops=4 * 10**9, bytes_accessed=10 << 20, transcendentals=0
        ),
    )(*inputs, projection, *consts)


def solution(mesh):
    return jax.shard_map(
        local,
        mesh=mesh,
        in_specs=(
            P("ctx", "tp"),
            P("ctx", "tp"),
            P("ctx", "tp"),
            P("ctx", None, "tp"),
            P("ctx", None, "tp"),
            P("ctx", "tp"),
        ),
        out_specs=P("ctx", "tp"),
        check_vma=False,
    )
```

```python
import functools
import math

import jax
import jax.numpy as jnp
import ml_dtypes
import numpy as np
from jax import lax
from jax.experimental import pallas as pl
from jax.experimental.pallas import tpu as pltpu
from jax.sharding import PartitionSpec as P

MESH = pl.DeviceIdType.MESH
BF = jnp.bfloat16
F32 = jnp.float32
Y_LOW = 2
CORES = 2
ROUNDS = 1
PARTS = 2
LEAD = 1


def cos_sin(grid, period):
    angles = grid.astype(np.float32) * np.float32(2.0 * math.pi / period)
    return np.cos(angles), np.sin(angles)


def tables(n, tok, cb):
    outer = 2 * n
    k, p, j = np.arange(outer), np.arange(n), np.arange(tok)
    bf = ml_dtypes.bfloat16
    co, so = (t.astype(bf).astype(np.float32) for t in cos_sin(k[:, None] * p[None, :], outer))
    ci, si = (t.astype(bf).astype(np.float32) for t in cos_sin(j[:, None] * j[None, :] % tok, tok))
    eye = np.eye(cb, dtype=np.float32)
    outer_fwd = np.concatenate([np.kron(co, eye), -np.kron(so, eye)], 0).astype(bf)
    outer_inv = np.ascontiguousarray(outer_fwd.T)
    inner_fwd = np.block([[ci, -si], [si, ci]]).astype(bf)
    inner_inv = np.block([[ci, si], [-si, ci]]).astype(bf)
    twid = np.stack([np.repeat(t, cb, 0) for t in cos_sin(k[:, None] * j[None, :], outer * tok)])
    return outer_fwd, outer_inv, inner_fwd, inner_inv, twid.astype(np.float32)


def peer(step, me, n):
    z_count = n // 2
    half, z = me // z_count, lax.rem(me, z_count)
    flip, u = lax.rem(step, 2), step // 2
    shift = jnp.where(lax.rem(u, 2) == 1, (u + 1) // 2, z_count - u // 2)
    return lax.rem(half + flip, 2) * z_count + lax.rem(z + shift, z_count)


def layer_kernel(
    n,
    groups,
    q_hbm,
    v_hbm,
    gate_hbm,
    sr_hbm,
    si_hbm,
    proj_hbm,
    wf_hbm,
    wi_hbm,
    mf_hbm,
    mi_hbm,
    tw_hbm,
    out_ref,
    q_ref,
    v_ref,
    gate_ref,
    sr_ref,
    si_ref,
    wf,
    wi,
    mf,
    mi,
    tw,
    sig_tx,
    sig_rx,
    spec_tx,
    spec_rx,
    freq,
    second,
    conv_tx,
    conv_rx,
    weights,
    feat_tx,
    feats,
    part_tx,
    part_rx,
    load_sem,
    send_sem,
    recv_sem,
    w_send,
    w_recv,
    f_send,
    f_recv,
    pair_sem,
    hand_sem,
    c_recv,
    lend_sem,
):
    me = lax.axis_index("ctx")
    mine = lax.axis_index("tp")
    tok, chan = q_ref.shape
    cb = chan // n
    sub = cb // ROUNDS
    rows = 2 * n * sub
    z_count = n // 2
    half, z = me // z_count, lax.rem(me, z_count)
    partner = (1 - half) * z_count + z
    x_count = groups // (Y_LOW * CORES)
    core = lax.rem(mine, CORES)
    y_low = lax.rem(mine // CORES, Y_LOW)
    x = mine // (CORES * Y_LOW)
    half_rows = proj_hbm.shape[0] // 2

    def group_at(dx, dy, dc):
        return (
            lax.rem(x + dx + x_count, x_count) * Y_LOW + lax.rem(y_low + dy, Y_LOW)
        ) * CORES + lax.rem(core + dc, CORES)

    near = []
    if x_count > 1:
        near += [group_at(1, 0, 0), group_at(-1, 0, 0)]
    if Y_LOW > 1:
        near.append(group_at(0, 1, 0))
    if CORES > 1:
        near.append(group_at(0, 0, 1))

    barrier = pltpu.get_barrier_semaphore()

    @pl.loop(1, n)
    def _(s):
        pl.semaphore_signal(barrier, inc=1, device_id={"ctx": peer(s, me, n)}, device_id_type=MESH)

    for other in near:
        pl.semaphore_signal(barrier, inc=1, device_id={"tp": other}, device_id_type=MESH)

    def proj_part(g, part):
        size = chan // PARTS
        return proj_hbm.at[
            pl.ds(pl.multiple_of(g * half_rows, half_rows), half_rows),
            part * size : (part + 1) * size,
        ]

    pairs = (
        (q_hbm, q_ref),
        (v_hbm, v_ref),
        (proj_part(half, 0), weights.at[0, me]),
        (proj_part(half, 1), weights.at[1, me]),
        (sr_hbm, sr_ref),
        (si_hbm, si_ref),
        (gate_hbm, gate_ref),
        (wf_hbm, wf),
        (tw_hbm, tw),
        (mf_hbm, mf),
        (mi_hbm, mi),
        (wi_hbm, wi),
    )
    loads = [pltpu.make_async_copy(a, b, load_sem.at[i]) for i, (a, b) in enumerate(pairs)]
    for load in loads:
        load.start()

    def exchange(kind, tx, rx, dest):
        return pltpu.make_async_remote_copy(
            src_ref=tx.at[dest],
            dst_ref=rx.at[me],
            send_sem=send_sem.at[kind],
            recv_sem=recv_sem.at[kind],
            device_id={"ctx": dest},
            device_id_type=MESH,
        )

    def send_all(kind, tx, rx):
        @pl.loop(1, n)
        def _(s):
            exchange(kind, tx, rx, peer(s, me, n)).start()

    def whole(ref, sem):
        return pltpu.make_async_copy(ref, ref, sem)

    def recv_all(kind, tx, rx):
        whole(rx.at[pl.ds(0, n - 1)], recv_sem.at[kind]).wait()

    def drain(kind, tx, rx):
        whole(tx.at[pl.ds(0, n - 1)], send_sem.at[kind]).wait()

    def reach(kind, way):
        return z_count // 2 - (kind + way) % 2

    def ring_copy(kind, way, d, part):
        sign = 1 - 2 * way
        owner = (half if kind == 0 else 1 - half) * z_count + lax.rem(
            z - sign * d + z_count, z_count
        )
        dest = half * z_count + lax.rem(z + sign + z_count, z_count)
        return pltpu.make_async_remote_copy(
            src_ref=weights.at[part, owner],
            dst_ref=weights.at[part, owner],
            send_sem=w_send.at[way],
            recv_sem=w_recv.at[part, owner],
            device_id={"ctx": dest},
            device_id_type=MESH,
        )

    def ring_step(d, kind, part):
        if d == 0 and kind == 0:
            loads[2 + part].wait()
        if d == 0 and kind == 1:
            ring_copy(1, 0, 0, part).wait_recv()
        for way in range(2):
            if 1 <= d <= reach(kind, way):
                ring_copy(kind, way, d, part).wait_recv()
            if d < reach(kind, way):
                ring_copy(kind, way, d, part).start()

    steps = z_count // 2 + 1
    ring_todo = [
        (i - LEAD * part, kind, part)
        for i in range(steps + LEAD)
        for part in range(PARTS)
        for kind in range(2)
        if 0 <= i - LEAD * part < steps
    ]
    lends = [
        pltpu.make_async_remote_copy(
            src_ref=proj_part(1 - half, part),
            dst_ref=weights.at[part, me],
            send_sem=lend_sem.at[part],
            recv_sem=w_recv.at[part, me],
            device_id={"ctx": partner},
            device_id_type=MESH,
        )
        for part in range(PARTS)
    ]

    def ring(count):
        for _ in range(min(count, len(ring_todo))):
            ring_step(*ring_todo.pop(0))

    def by_owner(values):
        return values.T.reshape(n, sub, tok)

    def spec_turn(r):
        cols = slice(r * n * sub, (r + 1) * n * sub)
        for part, ref in enumerate((sr_ref, si_ref)):
            both = [by_owner(ref[k, :, cols].astype(F32)) for k in range(2)]
            at = 2 * part * sub
            spec_tx[r, :, at : at + 2 * sub, :] = jnp.concatenate(both, axis=1).astype(BF)
        spec_rx[r, pl.ds(me, 1)] = spec_tx[r, pl.ds(me, 1)]

    def spec_send(r):
        send_all(1 + r, spec_tx.at[r], spec_rx.at[r])

    loads[0].wait()
    loads[1].wait()
    signal = q_ref[...].astype(F32) * v_ref[...].astype(F32)
    sig_tx[...] = jnp.concatenate(
        [by_owner(signal[:, r * n * sub : (r + 1) * n * sub]) for r in range(ROUNDS)], axis=1
    ).astype(BF)
    pl.semaphore_wait(barrier, n - 1 + len(near))
    send_all(0, sig_tx, sig_rx)
    for lend in lends:
        lend.start()
    step = 16 * sub
    chunks = rows // step

    def forward():
        recv_all(0, sig_tx, sig_rx)
        drain(0, sig_tx, sig_rx)
        sig_rx[pl.ds(me, 1)] = sig_tx[pl.ds(me, 1)]
        for load in loads[6:]:
            load.wait()
        for r in range(ROUNDS):
            block = sig_rx[...].astype(F32)[:, r * sub : (r + 1) * sub]
            second[: n * sub, :] = block.reshape(n * sub, tok).astype(BF)

            @pl.loop(0, chunks)
            def _(i):
                at = pl.ds(pl.multiple_of(i * step, step), step)
                lower = pl.ds(pl.multiple_of(rows + i * step, step), step)
                grid = second[: n * sub, :]
                real = jnp.dot(wf[at, :], grid, preferred_element_type=F32)
                imag = jnp.dot(wf[lower, :], grid, preferred_element_type=F32)
                u, w = tw[0, at, :], tw[1, at, :]
                first = jnp.concatenate(
                    [(real * u + imag * w).astype(BF), (imag * u - real * w).astype(BF)], axis=1
                )
                freq[r, at, :] = jnp.dot(first, mf[...], preferred_element_type=F32)

    scale = 1.0 / (2 * n * tok)
    side = tok // ROUNDS

    def filter_round(r):
        recv_all(1 + r, spec_tx.at[r], spec_rx.at[r])

        @pl.loop(0, chunks)
        def _(i):
            at = pl.ds(pl.multiple_of(i * step, step), step)
            lower = pl.ds(pl.multiple_of(rows + i * step, step), step)
            gain = spec_rx[r, pl.ds(i * 8, 8)].astype(F32)
            gain_r = gain[:, : 2 * sub].reshape(step, tok)
            gain_i = gain[:, 2 * sub :].reshape(step, tok)
            real, imag = freq[r, at, :tok], freq[r, at, tok:]
            filt = jnp.concatenate(
                [
                    (real * gain_r - imag * gain_i).astype(BF),
                    (real * gain_i + imag * gain_r).astype(BF),
                ],
                axis=1,
            )
            back = jnp.dot(filt, mi[...], preferred_element_type=F32)
            real, imag = back[:, :tok], back[:, tok:]
            u, w = tw[0, at, :], tw[1, at, :]
            second[at, :] = (real * u - imag * w).astype(BF)
            second[lower, :] = (imag * u + real * w).astype(BF)

        conv = jnp.dot(wi[...], second[...], preferred_element_type=F32) * scale
        conv = conv.reshape(n, sub, tok)
        conv_tx[r] = jnp.concatenate(
            [conv[:, :, i * side : (i + 1) * side] for i in range(ROUNDS)], axis=1
        ).astype(BF)
        send_all(1 + ROUNDS + r, conv_tx.at[r], conv_rx.at[r])
        conv_rx[r, pl.ds(me, 1)] = conv_tx[r, pl.ds(me, 1)]

    quarter = chan // 4
    blocks = 2 // ROUNDS
    hands = []

    def gated_half(r, g):
        parts = []
        for i in range(blocks):
            first = i * 2 * quarter + g * quarter
            conv = conv_rx[r, pl.ds(first // sub, quarter // sub)].astype(F32)
            cols = pl.ds(pl.multiple_of(r * 2 * quarter + first, quarter), quarter)
            gated = []
            for p in range(ROUNDS):
                turned = conv[:, p * sub : (p + 1) * sub].reshape(quarter, side).T
                gate = gate_ref[p * side : (p + 1) * side, cols].astype(F32)
                gated.append((turned * gate).astype(BF))
            parts.append(jnp.concatenate(gated, axis=0))
        return jnp.concatenate(parts, axis=1)

    def feat_copy(route, w, r, owner):
        dest = group_at(*((0, 1, 0), (1, 0, 0), (-1, 0, 0), (0, 0, 1))[route])
        return pltpu.make_async_remote_copy(
            src_ref=feats.at[w, r, owner],
            dst_ref=feats.at[w, r, owner],
            send_sem=f_send.at[r],
            recv_sem=c_recv.at[r] if route == 3 else f_recv.at[w, r, owner],
            device_id={"tp": dest},
            device_id_type=MESH,
        )

    sent = [0] * ROUNDS
    order = [(0, 0)]
    if Y_LOW > 1:
        order.append((0, 1))
    if x_count > 1:
        order += [(dx, dy) for dy in range(Y_LOW) for dx in (-1, 1)]
        order += [(2, dy) for dy in range(Y_LOW)]
    todo = [[(i, w) for i in range(len(order)) for w in range(2)] for _ in range(ROUNDS)]

    def relay(r, i, w):
        dx, dy = order[i]
        owner = group_at(dx, dy, 0)
        routes = []
        if i == 0 and Y_LOW > 1:
            routes.append(0)
        if dx == 0 and x_count > 1:
            routes += [1, 2]
        if dx == -1 and (w + dy) % 2 == 0:
            routes.append(1)
        if dx == 1 and (w + dy) % 2 == 1:
            routes.append(2)
        if CORES > 1:
            routes.append(3)
        if i > 0 or w > 0:
            feat_copy(0, w, r, owner).wait_recv()
        for route in routes:
            feat_copy(route, w, r, owner).start()
            sent[r] += 1

    def relays(r, count):
        for _ in range(min(count, len(todo[r]))):
            relay(r, *todo[r].pop(0))

    def features(r):
        recv_all(1 + ROUNDS + r, conv_tx.at[r], conv_rx.at[r])
        feat_tx[r] = gated_half(r, 1 - half)
        hand = pltpu.make_async_remote_copy(
            src_ref=feat_tx.at[r],
            dst_ref=feats.at[1, r, mine],
            send_sem=hand_sem.at[r],
            recv_sem=f_recv.at[1, r, mine],
            device_id={"ctx": partner},
            device_id_type=MESH,
        )
        hand.start()
        hands.append(hand)
        feats[0, r, pl.ds(mine, 1)] = gated_half(r, half)[None]
        relays(r, 1)

    loads[4].wait()
    loads[5].wait()
    spec_turn(0)
    spec_send(0)
    forward()
    ring(6)
    filter_round(0)
    drain(1, spec_tx.at[0], spec_rx.at[0])
    ring(6)
    features(0)
    ring(6)
    relays(0, 2)
    ring(2)
    relays(0, 2)
    ring(2)
    relays(0, 2)
    ring(2)
    relays(0, 2)
    ring(2)
    relays(0, 2)
    ring(2)
    relays(0, 2)
    ring(2)
    relays(0, 2)
    ring(2)
    relays(0, 2)
    ring(2)
    relays(0, 99)
    if CORES > 1:
        for r in range(ROUNDS):
            whole(feats.at[:, r, pl.ds(0, groups // 2)], c_recv.at[r]).wait()

    def product(w, part):
        left = jnp.concatenate([feats[w, 0, t] for t in range(groups)], axis=1)
        right = weights[part].reshape(n * half_rows, chan // PARTS)
        return jnp.dot(left, right, preferred_element_type=F32)

    swaps = []
    for part in range(PARTS):
        if part == PARTS - 1:
            ring(99)
        part_tx[part] = product(1, part).astype(BF)
        swap = pltpu.make_async_remote_copy(
            src_ref=part_tx.at[part],
            dst_ref=part_rx.at[part],
            send_sem=pair_sem.at[0, part],
            recv_sem=pair_sem.at[1, part],
            device_id={"ctx": partner},
            device_id_type=MESH,
        )
        swap.start()
        swaps.append(swap)
    size = chan // PARTS
    totals = [product(0, part) for part in range(PARTS)]
    for part, swap in enumerate(swaps):
        swap.wait_recv()
        out_ref[:, part * size : (part + 1) * size] = (
            totals[part] + part_rx[part].astype(F32)
        ).astype(BF)

    for r in range(ROUNDS):
        drain(1 + ROUNDS + r, conv_tx.at[r], conv_rx.at[r])
    for way in range(2):
        whole(weights.at[:, pl.ds(0, z_count - 1)], w_send.at[way]).wait()
    for r in range(ROUNDS):
        whole(feats.at[:, r, pl.ds(0, sent[r] // 2)], f_send.at[r]).wait()
    for lend in lends:
        lend.wait_send()
    for hand in hands:
        hand.wait_send()
    for swap in swaps:
        swap.wait_send()


def local(query_branch, value_branch, gate_branch, spectrum_real, spectrum_imag, projection):
    n, groups = lax.axis_size("ctx"), lax.axis_size("tp")
    tok, chan = query_branch.shape
    cb = chan // n
    sub = cb // ROUNDS
    rows = 2 * n * sub
    half_rows = projection.shape[0] // 2
    consts = [jnp.asarray(t) for t in tables(n, tok, sub)]
    inputs = (query_branch, value_branch, gate_branch, spectrum_real, spectrum_imag)
    dma = pltpu.SemaphoreType.DMA
    return pl.pallas_call(
        functools.partial(layer_kernel, n, groups),
        out_shape=pltpu.VMEM((tok, chan), BF),
        in_specs=[pl.BlockSpec(memory_space=pl.ANY)] * 11,
        out_specs=pl.BlockSpec(memory_space=pltpu.VMEM),
        scratch_shapes=[pltpu.VMEM(t.shape, t.dtype) for t in inputs]
        + [pltpu.VMEM(t.shape, t.dtype) for t in consts]
        + [
            pltpu.VMEM((n, cb, tok), BF),
            pltpu.VMEM((n, cb, tok), BF),
            pltpu.VMEM((ROUNDS, n, 4 * sub, tok), BF),
            pltpu.VMEM((ROUNDS, n, 4 * sub, tok), BF),
            pltpu.VMEM((ROUNDS, rows, 2 * tok), F32),
            pltpu.VMEM((2 * rows, tok), BF),
            pltpu.VMEM((ROUNDS, n, cb, tok // ROUNDS), BF),
            pltpu.VMEM((ROUNDS, n, cb, tok // ROUNDS), BF),
            pltpu.VMEM((PARTS, n, half_rows, chan // PARTS), BF),
            pltpu.VMEM((ROUNDS, tok, chan // 2 // ROUNDS), BF),
            pltpu.VMEM((2, ROUNDS, groups, tok, chan // 2 // ROUNDS), BF),
            pltpu.VMEM((PARTS, tok, chan // PARTS), BF),
            pltpu.VMEM((PARTS, tok, chan // PARTS), BF),
            dma((12,)),
            dma((1 + 2 * ROUNDS,)),
            dma((1 + 2 * ROUNDS,)),
            dma((2,)),
            dma((PARTS, n)),
            dma((ROUNDS,)),
            dma((2, ROUNDS, groups)),
            dma((2, PARTS)),
            dma((ROUNDS,)),
            dma((ROUNDS,)),
            dma((PARTS,)),
        ],
        compiler_params=pltpu.CompilerParams(
            collective_id=0, has_side_effects=True, vmem_limit_bytes=60 << 20
        ),
        cost_estimate=pl.CostEstimate(
            flops=4 * 10**9, bytes_accessed=10 << 20, transcendentals=0
        ),
    )(*inputs, projection, *consts)


def solution(mesh):
    return jax.shard_map(
        local,
        mesh=mesh,
        in_specs=(
            P("ctx", "tp"),
            P("ctx", "tp"),
            P("ctx", "tp"),
            P("ctx", None, "tp"),
            P("ctx", None, "tp"),
            P("ctx", "tp"),
        ),
        out_specs=P("ctx", "tp"),
        check_vma=False,
    )
```
